32 devices in a mesh: dp: 8 (over z, x), seq: 4 (over y, core).
Axes of the slice: x: 2, y: 2, z: 4, core: 2. Of those that a mesh axis runs over, the one named last changes fastest.
Arguments:
- hidden_in: bfloat16 [8, 1024, 1024], P('dp', 'seq'), may hold values from -6 to 6
- segments: int32 [8, 1024], P('dp'), may hold values from 0 to 2, as said below
- cotangent: bfloat16 [8, 1024, 1024], P('dp', 'seq'), may hold values from -6 to 6
- in_proj: bfloat16 [1024, 3352], P(('dp', 'seq')), may hold values from -0.1875 to 0.1875
- query_proj: bfloat16 [1024, 512], P(('dp', 'seq')), may hold values from -0.1875 to 0.1875
- key_proj: bfloat16 [1024, 128], P(('dp', 'seq')), may hold values from -0.1875 to 0.1875
- value_proj: bfloat16 [1024, 128], P(('dp', 'seq')), may hold values from -0.1875 to 0.1875
- attn_proj: bfloat16 [512, 1024], P(('dp', 'seq')), may hold values from -4 to 4
- mixer_proj: bfloat16 [1536, 1024], P(('dp', 'seq')), may hold values from -0.15625 to 0.15625
- gate_proj: bfloat16 [1024, 2048], P(('dp', 'seq')), may hold values from -0.1875 to 0.1875
- up_proj: bfloat16 [1024, 2048], P(('dp', 'seq')), may hold values from -0.1875 to 0.1875
- down_proj: bfloat16 [2048, 1024], P(('dp', 'seq')), may hold values from -0.125 to 0.125
- conv_weight: bfloat16 [1792, 4], P(('dp', 'seq')), may hold values from -3 to 3
- conv_bias: bfloat16 [1792], P(('dp', 'seq')), may hold values from -1.5 to 1.5
- norm_one: bfloat16 [1024], P(('dp', 'seq')), may hold values from 0.5 to 1.5
- norm_two: bfloat16 [1024], P(('dp', 'seq')), may hold values from 0.5 to 1.5
- mixer_norm: bfloat16 [1536], P(('dp', 'seq')), may hold values from 0.5 to 1.5
- step_bias: float32 [24], replicated, may hold values from -3.5 to -2.5
- decay_log: float32 [24], replicated, may hold values from -6 to -1
- skip_gain: float32 [24], replicated, may hold values from 0.5 to 1.5
Outputs:
- layer_out: bfloat16 [8, 1024, 1024], P('dp', 'seq')
- input_grad: float32 [8, 1024, 1024], P('dp', 'seq')
- in_proj_grad: float32 [1024, 3352], P(('dp', 'seq'))
- query_proj_grad: float32 [1024, 512], P(('dp', 'seq'))
- key_proj_grad: float32 [1024, 128], P(('dp', 'seq'))
- value_proj_grad: float32 [1024, 128], P(('dp', 'seq'))
- attn_proj_grad: float32 [512, 1024], P(('dp', 'seq'))
- mixer_proj_grad: float32 [1536, 1024], P(('dp', 'seq'))
- gate_proj_grad: float32 [1024, 2048], P(('dp', 'seq'))
- up_proj_grad: float32 [1024, 2048], P(('dp', 'seq'))
- down_proj_grad: float32 [2048, 1024], P(('dp', 'seq'))
- conv_weight_grad: float32 [1792, 4], P(('dp', 'seq'))
- conv_bias_grad: float32 [1792], P(('dp', 'seq'))
- norm_one_grad: float32 [1024], P(('dp', 'seq'))
- norm_two_grad: float32 [1024], P(('dp', 'seq'))
- mixer_norm_grad: float32 [1536], P(('dp', 'seq'))
- step_bias_grad: float32 [24], replicated
- decay_log_grad: float32 [24], replicated
- skip_gain_grad: float32 [24], replicated
The draws below stay inside these ranges and needn't reach their ends.
Inputs may be any that keep to these rules, and one draw needn't show every extreme that they name: Each sequence holds segments 0, 1 and 2 in order; segment 1 begins within the first half of 256 positions, segment 2 within the last half of 256 positions.
All inputs are finite; a program needn't handle non-finite values.
Results may differ from the reference program's by a relative error of at most 0.02.
Values may be sent and summed in bfloat16 or wider, within the bound.
A program may use at most 96 MiB of HBM per device.

```python
import jax
import jax.numpy as jnp
from jax import lax

D = 1024
H = 24
P_SIZE = 64
N = 128
CONV = 4
NH = 8
KVH = 2
HD = 64
FF = 2048
SEQ_LEN = 1024
SPAN = 256
BATCH = 8


def draw_segments(key, part):
    key = jax.random.fold_in(key, 7)
    first_key, second_key = jax.random.split(key)
    begin_one = jax.random.randint(first_key, (BATCH, 1), 1, SPAN // 2 + 1)
    begin_two = jax.random.randint(second_key, (BATCH, 1), SEQ_LEN - SPAN // 2, SEQ_LEN)
    places = jnp.arange(SEQ_LEN)[None, :]
    return (places >= begin_one).astype(jnp.int32) + (places >= begin_two).astype(jnp.int32)


def steps_of(rng, dims, shards, smallest, high):
    factor_of, own = 1.0, jax.random.fold_in(rng, 6)
    for axis_at, parts in shards:
        draws = jnp.exp(jax.random.uniform(jax.random.fold_in(own, axis_at), (parts,), jnp.float32, smallest / len(shards), high / len(shards)))
        factor_of = factor_of * jnp.repeat(draws, dims[axis_at] // parts).reshape([-1 if axis == axis_at else 1 for axis in range(len(dims))])
    return factor_of


def gaussian(own_key, shape, scale, limit, shards=(), dtype=jnp.bfloat16):
    drawn = scale * jax.random.normal(own_key, shape, jnp.float32)
    if shards:
        drawn = drawn * steps_of(own_key, shape, shards, -0.22, 0.18)
    return jnp.clip(drawn, -limit, limit).astype(dtype)


def setup_inputs(seed: int = 0) -> dict:
    key_of = jax.random.split(jax.random.key(seed), 21)
    hidden_in = gaussian(key_of[0], (BATCH, SEQ_LEN, D), 1.0, 6.0, ((0, 8), (1, 4)))
    segments = draw_segments(jax.random.fold_in(key_of[20], 71), 0)
    cotangent = gaussian(key_of[2], (BATCH, SEQ_LEN, D), 1.0, 6.0, ((0, 8), (1, 4)))
    in_proj = gaussian(key_of[3], (D, 2 * H * P_SIZE + 2 * N + H), D ** -0.5, 0.1875, ((0, 32),))
    query_proj = gaussian(key_of[4], (D, NH * HD), D ** -0.5, 0.1875, ((0, 32),))
    key_proj = gaussian(key_of[5], (D, KVH * HD), D ** -0.5, 0.1875, ((0, 32),))
    value_proj = gaussian(key_of[6], (D, KVH * HD), D ** -0.5, 0.1875, ((0, 32),))
    attn_proj = gaussian(key_of[7], (NH * HD, D), (max(1, SEQ_LEN // 512)) ** -0.5, 4.0, ((0, 32),))
    mixer_proj = gaussian(key_of[8], (H * P_SIZE, D), (H * P_SIZE) ** -0.5, 0.15625, ((0, 32),))
    gate_proj = gaussian(key_of[9], (D, FF), D ** -0.5, 0.1875, ((0, 32),))
    up_proj = gaussian(key_of[10], (D, FF), D ** -0.5, 0.1875, ((0, 32),))
    down_proj = gaussian(key_of[11], (FF, D), FF ** -0.5, 0.125, ((0, 32),))
    conv_weight = gaussian(key_of[12], (H * P_SIZE + 2 * N, CONV), CONV ** -0.5, 3.0, ((0, 32),))
    conv_bias = gaussian(key_of[13], (H * P_SIZE + 2 * N,), 0.3, 1.5, ((0, 32),))
    norm_one = jnp.clip(1.0 + 0.1 * jax.random.normal(key_of[14], (D,), jnp.float32), 0.5, 1.5).astype(jnp.bfloat16)
    norm_two = jnp.clip(1.0 + 0.1 * jax.random.normal(key_of[15], (D,), jnp.float32), 0.5, 1.5).astype(jnp.bfloat16)
    mixer_norm = jnp.clip(1.0 + 0.1 * jax.random.normal(key_of[16], (H * P_SIZE,), jnp.float32), 0.5, 1.5).astype(jnp.bfloat16)
    step_bias = jnp.clip(jax.random.uniform(key_of[17], (H,), jnp.float32, -3.5, -2.5), -3.5, -2.5)
    decay_log = jnp.clip(jax.random.uniform(key_of[18], (H,), jnp.float32, -6.0, -1.0), -6.0, -1.0)
    skip_gain = jnp.clip(jax.random.uniform(key_of[19], (H,), jnp.float32, 0.5, 1.5), 0.5, 1.5)
    return dict(hidden_in=hidden_in, segments=segments, cotangent=cotangent, in_proj=in_proj, query_proj=query_proj, key_proj=key_proj, value_proj=value_proj, attn_proj=attn_proj, mixer_proj=mixer_proj, gate_proj=gate_proj, up_proj=up_proj, down_proj=down_proj, conv_weight=conv_weight, conv_bias=conv_bias, norm_one=norm_one, norm_two=norm_two, mixer_norm=mixer_norm, step_bias=step_bias, decay_log=decay_log, skip_gain=skip_gain)


@jax.custom_vjp
def low(v):
    return lax.optimization_barrier(v.astype(jnp.bfloat16)).astype(jnp.float32)

@jax.custom_vjp
def low_back(v):
    return v

def low_keep(v):
    return (low(v), None)

def low_pass(kept, grad):
    return (grad,)

def back_keep(v):
    return (v, None)

def back_low(kept, grad):
    return (low(grad),)
low.defvjp(low_keep, low_pass)
low_back.defvjp(back_keep, back_low)
epsilon = 1e-05
highest = lax.Precision.HIGHEST

def matmul(left_side, right_side):
    return jnp.dot(left_side, right_side, precision=highest, preferred_element_type=jnp.float32)

def rms_scale(values, gain_vec):
    return values * lax.rsqrt(lax.optimization_barrier(jnp.mean(values * values, axis=-1, keepdims=True)) + epsilon) * gain_vec

def conv_silu(conv_in, segment_ids, conv_weight, conv_bias):
    length_here = conv_in.shape[0]
    padded = jnp.concatenate([jnp.zeros((CONV - 1, conv_in.shape[1]), jnp.float32), conv_in], axis=0)
    padded_ids = jnp.concatenate([jnp.full((CONV - 1,), -1, jnp.int32), segment_ids])
    running = conv_bias
    for offset in range(CONV):
        tap_mask = (padded_ids[offset:offset + length_here] == segment_ids).astype(jnp.float32)
        running = running + conv_weight[:, offset] * padded[offset:offset + length_here] * tap_mask[:, None]
    return jax.nn.silu(running)

def scan_mixer(conv_out, gate_z, step_raw, segment_ids, step_bias, decay_log, skip_gain, mixer_gain):
    length_here = conv_out.shape[0]
    head_input = conv_out[:, :H * P_SIZE].reshape(length_here, H, P_SIZE)
    write_vec = conv_out[:, H * P_SIZE:H * P_SIZE + N]
    read_vec = conv_out[:, H * P_SIZE + N:]
    step_size = jax.nn.softplus(step_raw + step_bias)
    log_decay = jnp.cumsum(step_size * -jnp.exp(decay_log), axis=0)
    places = jnp.arange(length_here)
    allowed = (segment_ids[:, None] == segment_ids[None, :]) & (places[:, None] >= places[None, :])
    log_gap = jnp.where(allowed[:, :, None], log_decay[:, None, :] - log_decay[None, :, :], -10000.0)
    mixing = jnp.exp(log_gap) * matmul(read_vec, write_vec.T)[:, :, None] * step_size[None, :, :]
    result = jnp.einsum('tuh,uhp->thp', mixing, head_input, precision=highest) + skip_gain[:, None] * head_input
    gated = result.reshape(length_here, H * P_SIZE) * jax.nn.silu(gate_z)
    return rms_scale(gated, mixer_gain)

def attend(query, keys, values, segment_ids):
    length_here = query.shape[0]
    group_size = NH // KVH
    query_heads = query.reshape(length_here, KVH, group_size, HD)
    key_heads = keys.reshape(length_here, KVH, HD)
    value_heads = values.reshape(length_here, KVH, HD)
    scores = low_back(jnp.einsum('tkgd,ukd->kgtu', query_heads, key_heads, precision=highest) * HD ** (-0.5))
    places = jnp.arange(length_here)
    allowed = (segment_ids[:, None] == segment_ids[None, :]) & (places[:, None] >= places[None, :])
    attn_probs = jax.nn.softmax(jnp.where(allowed, scores, -1e+30), axis=-1)
    mixed = jnp.einsum('kgtu,ukd->tkgd', low(attn_probs), value_heads, precision=highest)
    return low_back(low(mixed)).reshape(length_here, NH * HD)

def layer(params, hidden_f, segment_ids):
    in_proj, query_proj, key_proj, value_proj, attn_proj, mixer_proj, gate_proj, up_proj, down_proj, conv_weight, conv_bias, norm_one, norm_two, mixer_norm, step_bias, decay_log, skip_gain = params
    normed = low(rms_scale(hidden_f, norm_one))
    projected = low_back(low(matmul(normed, in_proj)))
    gate_z = projected[:, :H * P_SIZE]
    conv_in = projected[:, H * P_SIZE:2 * H * P_SIZE + 2 * N]
    step_raw = projected[:, 2 * H * P_SIZE + 2 * N:]
    conv_out = conv_silu(conv_in, segment_ids, conv_weight, conv_bias)
    mixed = low(scan_mixer(conv_out, gate_z, step_raw, segment_ids, step_bias, decay_log, skip_gain, mixer_norm))
    mixer_out = low_back(matmul(mixed, mixer_proj))
    query = low_back(low(matmul(normed, query_proj)))
    keys = low_back(low(matmul(normed, key_proj)))
    values = low_back(low(matmul(normed, value_proj)))
    attn_mix = attend(query, keys, values, segment_ids)
    attn_out = low_back(matmul(attn_mix, attn_proj))
    resid = hidden_f + mixer_out + attn_out
    normed_two = low(rms_scale(resid, norm_two))
    gate_val = low_back(matmul(normed_two, gate_proj))
    up_val = low_back(matmul(normed_two, up_proj))
    activated = low(jax.nn.silu(gate_val) * up_val)
    return resid + low_back(matmul(activated, down_proj))

def reference(hidden_in, segments, cotangent, in_proj, query_proj, key_proj, value_proj, attn_proj, mixer_proj, gate_proj, up_proj, down_proj, conv_weight, conv_bias, norm_one, norm_two, mixer_norm, step_bias, decay_log, skip_gain):
    params = (in_proj.astype(jnp.float32), query_proj.astype(jnp.float32), key_proj.astype(jnp.float32), value_proj.astype(jnp.float32), attn_proj.astype(jnp.float32), mixer_proj.astype(jnp.float32), gate_proj.astype(jnp.float32), up_proj.astype(jnp.float32), down_proj.astype(jnp.float32), conv_weight.astype(jnp.float32), conv_bias.astype(jnp.float32), norm_one.astype(jnp.float32), norm_two.astype(jnp.float32), mixer_norm.astype(jnp.float32), step_bias.astype(jnp.float32), decay_log.astype(jnp.float32), skip_gain.astype(jnp.float32))

    def one_sequence(totals, item):
        hidden_seq, segment_seq, cot_seq = item

        def forward(param_set, hidden_f):
            return layer(param_set, hidden_f, segment_seq)
        result, pullback = jax.vjp(forward, params, hidden_seq.astype(jnp.float32))
        param_grads, hidden_grad = pullback(cot_seq.astype(jnp.float32))
        totals = jax.tree.map(lambda running, fresh: running + fresh, totals, param_grads)
        return (totals, (result.astype(jnp.bfloat16), hidden_grad))
    zero_grads = jax.tree.map(jnp.zeros_like, params)
    totals, (layer_out, input_grad) = lax.scan(one_sequence, zero_grads, (hidden_in, segments, cotangent))
    return (layer_out, input_grad, totals[0], totals[1], totals[2], totals[3], totals[4], totals[5], totals[6], totals[7], totals[8], totals[9], totals[10], totals[11], totals[12], totals[13], totals[14], totals[15], totals[16])
```

```python
import functools

import jax
import jax.numpy as jnp
from jax import lax
from jax.experimental import pallas as pl
from jax.experimental.pallas import tpu as pltpu
from jax.sharding import PartitionSpec as P

H = 24
P_SIZE = 64
N = 128
CONV = 4
NH = 8
KVH = 2
HD = 64
INNER = H * P_SIZE
CONV_W = INNER + 2 * N
Q_AT = INNER + CONV_W
K_AT = Q_AT + NH * HD
V_AT = K_AT + KVH * HD
RAW_AT = V_AT + KVH * HD
PACK = RAW_AT + H
BOTH = ("dp", "seq")
EPS = 1e-05
F32 = jnp.float32
BF = jnp.bfloat16
EXACT = lax.Precision.HIGHEST
VMEM = 48 * 1024 * 1024
SCALE = HD ** (-0.5)


def dot(a, b):
    return jnp.dot(a, b, preferred_element_type=F32)


def dot_ta(a, b):
    return lax.dot_general(a, b, (((0,), (0,)), ((), ())), preferred_element_type=F32)


def dot_tb(a, b):
    return lax.dot_general(a, b, (((1,), (1,)), ((), ())), preferred_element_type=F32)


def exact_dot(a, b):
    return jnp.dot(a, b, precision=EXACT, preferred_element_type=F32)


def gather_all(a):
    return lax.all_gather(a, BOTH, axis=0, tiled=True)


def scatter_all(a):
    return lax.psum_scatter(a.astype(BF), BOTH, scatter_dimension=0, tiled=True).astype(F32)


def column_of(block, at):
    lanes = lax.broadcasted_iota(jnp.int32, block.shape, 1)
    return jnp.sum(jnp.where(lanes == at, block, 0.0), axis=1, keepdims=True)


def decay_between(log_ref, log_row_ref, seg_col_ref, seg_row_ref, head):
    rows = log_ref.shape[0]
    at_row = lax.broadcasted_iota(jnp.int32, (rows, rows), 0)
    at_col = lax.broadcasted_iota(jnp.int32, (rows, rows), 1)
    allowed = (at_row >= at_col) & (seg_col_ref[...] == seg_row_ref[...])
    gap = column_of(log_ref[...], head) - log_row_ref[pl.ds(head, 1), :]
    return jnp.exp(jnp.where(allowed, gap, -10000.0))


def inner_forward_kernel(x_ref, g_ref, log_ref, log_row_ref, dt_row_ref, sc_ref, sr_ref, y_ref):
    pair = pl.program_id(0)
    x = x_ref[...]
    lanes = lax.broadcasted_iota(jnp.int32, x.shape, 1)
    parts = []
    for i in range(2):
        head = 2 * pair + i
        e = decay_between(log_ref, log_row_ref, sc_ref, sr_ref, head)
        mixing = (e * dt_row_ref[pl.ds(head, 1), :] * g_ref[...]).astype(BF)
        parts.append(dot(mixing, x))
    y_ref[...] = jnp.where(lanes < P_SIZE, parts[0], parts[1])


def inner_backward_kernel(
    x_ref, dy_ref, g_ref, log_ref, log_row_ref, dt_row_ref, sc_ref, sr_ref,
    dx_ref, dg_ref, row_ref, col_ref,
):
    pair = pl.program_id(0)

    @pl.when(pair == 0)
    def _():
        dg_ref[...] = jnp.zeros_like(dg_ref)
        row_ref[...] = jnp.zeros_like(row_ref)

    x = x_ref[...]
    dy = dy_ref[...]
    lanes = lax.broadcasted_iota(jnp.int32, x.shape, 1)
    row_lanes = lax.broadcasted_iota(jnp.int32, row_ref.shape, 1)
    parts = []
    for i in range(2):
        head = 2 * pair + i
        e = decay_between(log_ref, log_row_ref, sc_ref, sr_ref, head)
        dt = dt_row_ref[pl.ds(head, 1), :]
        g = g_ref[...]
        mine = (lanes < P_SIZE) if i == 0 else (lanes >= P_SIZE)
        dm = dot_tb(jnp.where(mine, dy, jnp.zeros_like(dy)), x)
        q = dm * e
        eg = e * g
        parts.append(dot_ta((eg * dt).astype(BF), dy))
        qd = q * dt
        dg_ref[...] += qd
        row_ref[...] += jnp.where(
            row_lanes == head, jnp.sum(qd * g, axis=1, keepdims=True), 0.0
        )
        col_ref[pl.ds(head, 1), :] = jnp.sum(q * g, axis=0, keepdims=True)
    dx_ref[...] = jnp.where(lanes < P_SIZE, parts[0], parts[1])


def whole(shape):
    return pl.BlockSpec(shape, lambda p: (0,) * len(shape))


def pair_block(rows):
    return pl.BlockSpec((rows, 2 * P_SIZE), lambda p: (0, p))


def params():
    return pltpu.CompilerParams(vmem_limit_bytes=VMEM)


def inner_forward(x, g, log_col, log_row, dt_row, seg_col, seg_row):
    t = x.shape[0]
    return pl.pallas_call(
        inner_forward_kernel,
        grid=(H // 2,),
        in_specs=[
            pair_block(t), whole((t, t)), whole((t, H)), whole((H, t)), whole((H, t)),
            whole((t, 1)), whole((1, t)),
        ],
        out_specs=pair_block(t),
        out_shape=jax.ShapeDtypeStruct((t, INNER), F32),
        compiler_params=params(),
        cost_estimate=pl.CostEstimate(
            flops=4 * H * t * t * P_SIZE, bytes_accessed=6 * t * INNER, transcendentals=H * t * t
        ),
    )(x, g, log_col, log_row, dt_row, seg_col, seg_row)


def inner_backward(x, dy, g, log_col, log_row, dt_row, seg_col, seg_row):
    t = x.shape[0]
    return pl.pallas_call(
        inner_backward_kernel,
        grid=(H // 2,),
        in_specs=[
            pair_block(t), pair_block(t), whole((t, t)), whole((t, H)), whole((H, t)),
            whole((H, t)), whole((t, 1)), whole((1, t)),
        ],
        out_specs=[pair_block(t), whole((t, t)), whole((t, H)), whole((H, t))],
        out_shape=[
            jax.ShapeDtypeStruct((t, INNER), F32),
            jax.ShapeDtypeStruct((t, t), F32),
            jax.ShapeDtypeStruct((t, H), F32),
            jax.ShapeDtypeStruct((H, t), F32),
        ],
        compiler_params=params(),
        cost_estimate=pl.CostEstimate(
            flops=8 * H * t * t * P_SIZE, bytes_accessed=8 * t * INNER, transcendentals=H * t * t
        ),
    )(x, dy, g, log_col, log_row, dt_row, seg_col, seg_row)


def head_scores(q, k_ref, allowed, lanes, i):
    mine = (lanes < HD) if i == 0 else (lanes >= HD)
    own = jnp.where(mine, q, jnp.zeros_like(q))
    return mine, own, jnp.where(allowed, dot_tb(own, k_ref[...]) * SCALE, -1e30)


def keys_allowed(first, sc_ref, sr_ref):
    shape = (sc_ref.shape[0], sr_ref.shape[1])
    at_row = lax.broadcasted_iota(jnp.int32, shape, 0) + first
    at_col = lax.broadcasted_iota(jnp.int32, shape, 1)
    return (at_row >= at_col) & (sc_ref[...] == sr_ref[...])


def attend_forward_kernel(q_ref, k_ref, v_ref, sc_ref, sr_ref, out_ref, lse_ref):
    first = lax.axis_index("seq") * q_ref.shape[0]
    allowed = keys_allowed(first, sc_ref, sr_ref)
    q = q_ref[...]
    lanes = lax.broadcasted_iota(jnp.int32, q.shape, 1)
    outs, totals = [], []
    for i in range(2):
        _, _, scores = head_scores(q, k_ref, allowed, lanes, i)
        top = jnp.max(scores, axis=1, keepdims=True)
        probs = jnp.exp(scores - top)
        total = jnp.sum(probs, axis=1, keepdims=True)
        outs.append(dot(probs.astype(BF), v_ref[...]) / total)
        totals.append(top + jnp.log(total))
    out_ref[...] = jnp.where(lanes < HD, outs[0], outs[1]).astype(BF)
    lse_ref[...] = jnp.where(lanes < HD, totals[0], totals[1])


def attend_backward_kernel(
    q_ref, k_ref, v_ref, dm_ref, lse_ref, sc_ref, sr_ref, dq_ref, dk_ref, dv_ref
):
    pair = pl.program_id(0)

    @pl.when(lax.rem(pair, NH // KVH // 2) == 0)
    def _():
        dk_ref[...] = jnp.zeros_like(dk_ref)
        dv_ref[...] = jnp.zeros_like(dv_ref)

    first = lax.axis_index("seq") * q_ref.shape[0]
    allowed = keys_allowed(first, sc_ref, sr_ref)
    q = q_ref[...]
    dmix = dm_ref[...]
    lanes = lax.broadcasted_iota(jnp.int32, q.shape, 1)
    dqs = []
    for i in range(2):
        mine, own, scores = head_scores(q, k_ref, allowed, lanes, i)
        probs = jnp.exp(scores - lse_ref[:, i * HD : i * HD + 1])
        down = jnp.where(mine, dmix, jnp.zeros_like(dmix))
        dp = dot_tb(down, v_ref[...])
        delta = jnp.sum(probs * dp, axis=1, keepdims=True)
        ds = (probs * (dp - delta)).astype(BF)
        dqs.append(dot(ds, k_ref[...]) * SCALE)
        dk_ref[...] += dot_ta(ds, own) * SCALE
        dv_ref[...] += dot_ta(probs.astype(BF), down)
    dq_ref[...] = jnp.where(lanes < HD, dqs[0], dqs[1]).astype(BF)


def kv_block(keys):
    per = NH // KVH // 2
    return pl.BlockSpec((keys, 2 * HD), lambda p: (0, p // per))


def attend_forward(q, k2, v2, seg_col, seg_row):
    t, keys = q.shape[0], k2.shape[0]
    return pl.pallas_call(
        attend_forward_kernel,
        grid=(NH // 2,),
        in_specs=[
            pair_block(t), kv_block(keys), kv_block(keys), whole((t, 1)), whole((1, keys)),
        ],
        out_specs=[pair_block(t), pair_block(t)],
        out_shape=[
            jax.ShapeDtypeStruct((t, NH * HD), BF),
            jax.ShapeDtypeStruct((t, NH * HD), F32),
        ],
        compiler_params=params(),
        cost_estimate=pl.CostEstimate(
            flops=8 * NH * t * keys * HD, bytes_accessed=2 << 20, transcendentals=NH * t * keys
        ),
    )(q, k2, v2, seg_col, seg_row)


def attend_backward(q, k2, v2, dmix, lse, seg_col, seg_row):
    t, keys = q.shape[0], k2.shape[0]
    return pl.pallas_call(
        attend_backward_kernel,
        grid=(NH // 2,),
        in_specs=[
            pair_block(t), kv_block(keys), kv_block(keys), pair_block(t), pair_block(t),
            whole((t, 1)), whole((1, keys)),
        ],
        out_specs=[pair_block(t), kv_block(keys), kv_block(keys)],
        out_shape=[
            jax.ShapeDtypeStruct((t, NH * HD), BF),
            jax.ShapeDtypeStruct((keys, 2 * KVH * HD), F32),
            jax.ShapeDtypeStruct((keys, 2 * KVH * HD), F32),
        ],
        compiler_params=params(),
        cost_estimate=pl.CostEstimate(
            flops=20 * NH * t * keys * HD, bytes_accessed=4 << 20, transcendentals=NH * t * keys
        ),
    )(q, k2, v2, dmix, lse, seg_col, seg_row)


def doubled(pair):
    a, b = pair[:, :HD], pair[:, HD:]
    return jnp.concatenate([a, a, b, b], axis=1)


def folded(wide):
    parts = [wide[:, i * HD : (i + 1) * HD] for i in range(2 * KVH)]
    return jnp.concatenate([parts[0] + parts[1], parts[2] + parts[3]], axis=1)


def carried_states(everything, coefs, size):
    total = 0.0
    for k in range(size):
        part = everything[k].reshape(H, P_SIZE, N).astype(F32)
        total = total + coefs[k][:, None, None] * part
    return total.reshape(INNER, N)


def norm_back(values, scale, gain, grad):
    weighted = gain * grad
    return scale * weighted - values * scale**3 * jnp.mean(
        values * weighted, axis=-1, keepdims=True
    )


def body(
    hidden_in,
    segments,
    cotangent,
    in_proj,
    query_proj,
    key_proj,
    value_proj,
    attn_proj,
    mixer_proj,
    gate_proj,
    up_proj,
    down_proj,
    conv_weight,
    conv_bias,
    norm_one,
    norm_two,
    mixer_norm,
    step_bias,
    decay_log,
    skip_gain,
):
    size, here = lax.axis_size("seq"), lax.axis_index("seq")
    owners = size * lax.axis_size("dp")
    t = hidden_in.shape[1]
    seq_length = segments.shape[1]
    own_conv, own_d, own_in = conv_weight.shape[0], norm_one.shape[0], mixer_norm.shape[0]
    width = own_d * owners

    small = jnp.concatenate(
        [conv_weight.T.reshape(-1), conv_bias, norm_one, norm_two, mixer_norm]
    )
    small = lax.all_gather(small, BOTH, axis=0)
    in_pack = gather_all(
        jnp.concatenate(
            [in_proj[:, :Q_AT], query_proj, key_proj, value_proj, in_proj[:, Q_AT:]], axis=1
        )
    )
    full_mixer = gather_all(mixer_proj)
    full_attn = gather_all(attn_proj)
    full_gu = gather_all(jnp.concatenate([gate_proj, up_proj], axis=1))
    full_down = gather_all(down_proj)

    cut = (CONV + 1) * own_conv
    conv_all = (
        small[:, :cut]
        .reshape(owners, CONV + 1, own_conv)
        .transpose(1, 0, 2)
        .reshape(CONV + 1, CONV_W)
        .astype(F32)
    )
    gains = (
        small[:, cut : cut + 2 * own_d]
        .reshape(owners, 2, own_d)
        .transpose(1, 0, 2)
        .reshape(2, width)
        .astype(F32)
    )
    gain_one, gain_two = gains[0], gains[1]
    mixer_gain = small[:, cut + 2 * own_d :].reshape(INNER).astype(F32)

    segs = segments[0]
    first = here * t
    padded_ids = jnp.concatenate([jnp.full((CONV - 1,), -1, jnp.int32), segs])
    ext_ids = lax.dynamic_slice_in_dim(padded_ids, first, t + CONV - 1, 0)
    ids = ext_ids[CONV - 1 :]
    before = ext_ids[CONV - 2]
    taps = [(ext_ids[j : j + t] == ids).astype(F32)[:, None] for j in range(CONV)]
    seg_col, seg_row, seg_all = ids[:, None], ids[None, :], segs[None, :]
    to_end = (ids == ids[-1]).astype(F32)[:, None]
    from_before = (ids == before).astype(F32)[:, None]
    across = (ids[-1] == before).astype(F32)
    lower = jnp.tril(jnp.ones((t, t), F32))
    spread = jnp.repeat(jnp.eye(H, dtype=F32), P_SIZE, axis=1)

    hidden = hidden_in[0].astype(F32)
    scale_one = lax.rsqrt(jnp.mean(hidden * hidden, axis=-1, keepdims=True) + EPS)
    normed = (hidden * scale_one * gain_one).astype(BF)
    proj = dot(normed, in_pack).astype(BF)
    query = proj[:, Q_AT:K_AT]
    conv_in = proj[:, INNER:Q_AT]
    pairs = [(i, i + 1) for i in range(size - 1)]
    rim = lax.ppermute(conv_in[t - CONV + 1 :], "seq", pairs)
    kv = lax.all_gather(proj[:, K_AT:RAW_AT], "seq", axis=0, tiled=True)
    gate_z = proj[:, :INNER].astype(F32)
    step_in = proj[:, RAW_AT:].astype(F32) + step_bias
    ext = jnp.concatenate([rim, conv_in], axis=0).astype(F32)

    running = conv_all[CONV]
    for j in range(CONV):
        running = running + conv_all[j] * ext[j : j + t] * taps[j]
    conv_sig = jax.nn.sigmoid(running)
    conv_out = running * conv_sig
    x = conv_out[:, :INNER]
    x_low = x.astype(BF)
    write = conv_out[:, INNER : INNER + N].astype(BF)
    read = conv_out[:, INNER + N :].astype(BF)
    dt = jax.nn.softplus(step_in)
    rate = -jnp.exp(decay_log)
    log_decay = exact_dot(lower, dt * rate)
    log_row, dt_row = log_decay.T, dt.T
    end_bare = jnp.exp(log_decay[-1:] - log_decay) * to_end
    end_weight = end_bare * dt
    from_state = jnp.exp(log_decay) * from_before
    wide = exact_dot(jnp.concatenate([end_weight, from_state], axis=0), spread)
    end_wide, from_wide = wide[:t], wide[t:]
    skip_wide = jnp.repeat(skip_gain, P_SIZE)
    xw = (x * end_wide).astype(BF)
    state_local = dot_ta(xw, write)
    block_decay = jnp.exp(log_decay[-1]) * across
    decay_rows = jnp.pad(block_decay[None, :], ((0, 15), (0, N - H)))
    states = lax.all_gather(
        jnp.concatenate([state_local, decay_rows], axis=0).astype(BF), "seq", axis=0
    )
    decays = states[:, INNER, :H].astype(F32)
    ones = jnp.ones((H,), F32)
    fore, back = [None] * size, [None] * size
    run = ones
    for k in range(size - 1, -1, -1):
        inside = k < here
        fore[k] = jnp.where(inside, run, 0.0)
        run = jnp.where(inside, run * decays[k], run)
    run = ones
    for k in range(size):
        inside = k > here
        back[k] = jnp.where(inside, run, 0.0)
        run = jnp.where(inside, run * decays[k], run)
    state_f = carried_states(states[:, :INNER], fore, size)
    state_in = state_f.astype(BF)

    gram = dot_tb(read, write)
    inner = inner_forward(x_low, gram, log_decay, log_row, dt_row, seg_col, seg_row)
    from_read = dot_tb(read, state_in)
    ssm_out = inner + from_wide * from_read + skip_wide * x
    sig_z = jax.nn.sigmoid(gate_z)
    silu_z = gate_z * sig_z
    gated = ssm_out * silu_z
    scale_mix = lax.rsqrt(jnp.mean(gated * gated, axis=-1, keepdims=True) + EPS)
    mixed = (gated * scale_mix * mixer_gain).astype(BF)

    k2, v2 = doubled(kv[:, : KVH * HD]), doubled(kv[:, KVH * HD :])
    attn_mix, lse = attend_forward(query, k2, v2, seg_col, seg_all)
    resid = hidden + dot(mixed, full_mixer) + dot(attn_mix, full_attn)
    scale_two = lax.rsqrt(jnp.mean(resid * resid, axis=-1, keepdims=True) + EPS)
    normed_two = (resid * scale_two * gain_two).astype(BF)
    ff = full_gu.shape[1] // 2
    gate_up = dot(normed_two, full_gu)
    gate_val, up_val = gate_up[:, :ff], gate_up[:, ff:]
    sig_g = jax.nn.sigmoid(gate_val)
    activated = (gate_val * sig_g * up_val).astype(BF)
    layer_out = (resid + dot(activated, full_down)).astype(BF)

    cot = cotangent[0]
    down_w = scatter_all(dot_ta(activated, cot))
    act_grad = dot_tb(cot, full_down)
    gate_grad = act_grad * up_val * sig_g * (1.0 + gate_val * (1.0 - sig_g))
    up_grad = act_grad * gate_val * sig_g
    gu_grad = jnp.concatenate([gate_grad.astype(BF), up_grad.astype(BF)], axis=1)
    gu_w = scatter_all(dot_ta(normed_two, gu_grad))
    normed_two_grad = dot_tb(gu_grad, full_gu)
    two_grad = jnp.sum(resid * scale_two * normed_two_grad, axis=0)
    resid_grad = cot.astype(F32) + norm_back(resid, scale_two, gain_two, normed_two_grad)
    resid_low = resid_grad.astype(BF)
    mixed_grad = dot_tb(resid_low, full_mixer)
    mix_grad = dot_tb(resid_low, full_attn).astype(BF)

    gain_grad = jnp.sum(gated * scale_mix * mixed_grad, axis=0)
    gated_grad = norm_back(gated, scale_mix, mixer_gain, mixed_grad)
    out_grad = gated_grad * silu_z
    gate_z_grad = gated_grad * ssm_out * sig_z * (1.0 + gate_z * (1.0 - sig_z))
    out_low = out_grad.astype(BF)
    out_from = (out_grad * from_wide).astype(BF)
    state_grad = dot_ta(out_from, read).astype(BF)
    state_grads = lax.all_gather(state_grad, "seq", axis=0)

    query_grad, dk2, dv2 = attend_backward(query, k2, v2, mix_grad, lse, seg_col, seg_all)
    kv_grad = lax.psum_scatter(
        jnp.concatenate([folded(dk2), folded(dv2)], axis=1).astype(BF),
        "seq",
        scatter_dimension=0,
        tiled=True,
    )
    mixer_w = scatter_all(dot_ta(mixed, resid_low))
    attn_w = scatter_all(dot_ta(attn_mix, resid_low))

    inner_x, gram_grad, row_sum, col_sum = inner_backward(
        x_low, out_low, gram, log_decay, log_row, dt_row, seg_col, seg_row
    )
    gram_low = gram_grad.astype(BF)
    skip_grad = jnp.sum(jnp.sum(out_grad * x, axis=0).reshape(H, P_SIZE), axis=1)
    later_f = carried_states(state_grads, back, size)
    later = later_f.astype(BF)
    decay_grad = jnp.sum((later_f * state_f).reshape(H, P_SIZE * N), axis=1)
    from_write = dot_tb(write, later)
    x_grad = inner_x + skip_wide * out_grad + end_wide * from_write
    write_grad = dot_ta(gram_low, read) + dot(xw, later)
    read_grad = dot(gram_low, write) + dot(out_from, state_in)
    sums = exact_dot(
        jnp.concatenate([out_grad * from_read, x * from_write], axis=0), spread.T
    )
    from_grad, end_grad = sums[:t] * from_state, sums[t:]
    end_part = end_weight * end_grad
    dt_part = col_sum.T
    log_grad = row_sum - dt * dt_part + from_grad - end_part
    last = (jnp.arange(t) == t - 1).astype(F32)[:, None]
    log_grad = log_grad + last * (jnp.sum(end_part, axis=0) + block_decay * decay_grad)
    rate_grad = exact_dot(lower.T, log_grad)
    dt_grad = dt_part + end_bare * end_grad + rate_grad * rate
    decay_log_grad = jnp.sum(rate_grad * dt * rate, axis=0)
    raw_grad = dt_grad * jax.nn.sigmoid(step_in)
    step_bias_grad = jnp.sum(raw_grad, axis=0)

    conv_grad = jnp.concatenate([x_grad, write_grad, read_grad], axis=1)
    sum_grad = conv_grad * conv_sig * (1.0 + running * (1.0 - conv_sig))
    conv_b_grad = jnp.sum(sum_grad, axis=0)
    conv_w_grads = []
    ext_grad = 0.0
    for j in range(CONV):
        counted = sum_grad * taps[j]
        conv_w_grads.append(jnp.sum(counted * ext[j : j + t], axis=0))
        ext_grad = ext_grad + jnp.pad(counted * conv_all[j], ((j, CONV - 1 - j), (0, 0)))
    rim_grad = lax.ppermute(ext_grad[: CONV - 1], "seq", [(b, a) for a, b in pairs])
    conv_in_grad = ext_grad[CONV - 1 :] + jnp.pad(rim_grad, ((t - CONV + 1, 0), (0, 0)))
    pack_grad = jnp.concatenate(
        [
            gate_z_grad.astype(BF),
            conv_in_grad.astype(BF),
            query_grad,
            kv_grad,
            raw_grad.astype(BF),
        ],
        axis=1,
    )
    pack_w = scatter_all(dot_ta(normed, pack_grad))
    normed_grad = dot_tb(pack_grad, in_pack)
    one_grad = jnp.sum(hidden * scale_one * normed_grad, axis=0)
    input_grad = resid_grad + norm_back(hidden, scale_one, gain_one, normed_grad)

    conv_grads = jnp.stack(conv_w_grads + [conv_b_grad])
    norm_grads = jnp.stack([one_grad, two_grad])
    small_grad = jnp.concatenate(
        [
            conv_grads.reshape(CONV + 1, owners, own_conv).transpose(1, 0, 2).reshape(owners, cut),
            norm_grads.reshape(2, owners, own_d).transpose(1, 0, 2).reshape(owners, 2 * own_d),
            gain_grad.reshape(owners, own_in),
        ],
        axis=1,
    )
    small_own = scatter_all(small_grad)[0]
    head_sums = lax.psum(jnp.stack([step_bias_grad, decay_log_grad, skip_grad]), BOTH)
    taps_cut = CONV * own_conv
    return (
        layer_out[None],
        input_grad[None],
        jnp.concatenate([pack_w[:, :Q_AT], pack_w[:, RAW_AT:]], axis=1),
        pack_w[:, Q_AT:K_AT],
        pack_w[:, K_AT:V_AT],
        pack_w[:, V_AT:RAW_AT],
        attn_w,
        mixer_w,
        gu_w[:, :ff],
        gu_w[:, ff:],
        down_w,
        small_own[:taps_cut].reshape(CONV, own_conv).T,
        small_own[taps_cut:cut],
        small_own[cut : cut + own_d],
        small_own[cut + own_d : cut + 2 * own_d],
        small_own[cut + 2 * own_d :],
        head_sums[0],
        head_sums[1],
        head_sums[2],
    )


def solution(mesh):
    placed = (
        P("dp", "seq", None),
        P("dp", None),
        P("dp", "seq", None),
        P(("dp", "seq"), None),
        P(("dp", "seq"), None),
        P(("dp", "seq"), None),
        P(("dp", "seq"), None),
        P(("dp", "seq"), None),
        P(("dp", "seq"), None),
        P(("dp", "seq"), None),
        P(("dp", "seq"), None),
        P(("dp", "seq"), None),
        P(("dp", "seq"), None),
        P(("dp", "seq")),
        P(("dp", "seq")),
        P(("dp", "seq")),
        P(("dp", "seq")),
        P(),
        P(),
        P(),
    )
    return jax.shard_map(
        body,
        mesh=mesh,
        in_specs=placed,
        out_specs=(
            P("dp", "seq", None),
            P("dp", "seq", None),
            P(("dp", "seq"), None),
            P(("dp", "seq"), None),
            P(("dp", "seq"), None),
            P(("dp", "seq"), None),
            P(("dp", "seq"), None),
            P(("dp", "seq"), None),
            P(("dp", "seq"), None),
            P(("dp", "seq"), None),
            P(("dp", "seq"), None),
            P(("dp", "seq"), None),
            P(("dp", "seq")),
            P(("dp", "seq")),
            P(("dp", "seq")),
            P(("dp", "seq")),
            P(),
            P(),
            P(),
        ),
        check_vma=False,
    )
```

```python
import functools

import jax
import jax.numpy as jnp
from jax import lax
from jax.experimental import pallas as pl
from jax.experimental.pallas import tpu as pltpu
from jax.sharding import PartitionSpec as P

H = 24
P_SIZE = 64
N = 128
CONV = 4
NH = 8
KVH = 2
HD = 64
INNER = H * P_SIZE
CONV_W = INNER + 2 * N
Q_AT = INNER + CONV_W
K_AT = Q_AT + NH * HD
V_AT = K_AT + KVH * HD
RAW_AT = V_AT + KVH * HD
PACK = RAW_AT + H
BOTH = ("dp", "seq")
EPS = 1e-05
F32 = jnp.float32
BF = jnp.bfloat16
EXACT = lax.Precision.HIGHEST
VMEM = 48 * 1024 * 1024
SCALE = HD ** (-0.5)


def dot(a, b):
    return jnp.dot(a, b, preferred_element_type=F32)


def dot_ta(a, b):
    return lax.dot_general(a, b, (((0,), (0,)), ((), ())), preferred_element_type=F32)


def dot_tb(a, b):
    return lax.dot_general(a, b, (((1,), (1,)), ((), ())), preferred_element_type=F32)


def exact_dot(a, b):
    return jnp.dot(a, b, precision=EXACT, preferred_element_type=F32)


def gather_all(a):
    return lax.all_gather(a, BOTH, axis=0, tiled=True)


def scatter_all(a):
    return lax.psum_scatter(a.astype(BF), BOTH, scatter_dimension=0, tiled=True).astype(F32)


def column_of(block, at):
    lanes = lax.broadcasted_iota(jnp.int32, block.shape, 1)
    return jnp.sum(jnp.where(lanes == at, block, 0.0), axis=1, keepdims=True)


def decay_between(log_ref, log_row_ref, seg_col_ref, seg_row_ref, head):
    rows = log_ref.shape[0]
    at_row = lax.broadcasted_iota(jnp.int32, (rows, rows), 0)
    at_col = lax.broadcasted_iota(jnp.int32, (rows, rows), 1)
    allowed = (at_row >= at_col) & (seg_col_ref[...] == seg_row_ref[...])
    gap = column_of(log_ref[...], head) - log_row_ref[pl.ds(head, 1), :]
    return jnp.exp(jnp.where(allowed, gap, -10000.0))


def inner_forward_kernel(x_ref, g_ref, log_ref, log_row_ref, dt_row_ref, sc_ref, sr_ref, y_ref):
    pair = pl.program_id(0)
    x = x_ref[...]
    lanes = lax.broadcasted_iota(jnp.int32, x.shape, 1)
    parts = []
    for i in range(2):
        head = 2 * pair + i
        e = decay_between(log_ref, log_row_ref, sc_ref, sr_ref, head)
        mixing = (e * dt_row_ref[pl.ds(head, 1), :] * g_ref[...]).astype(BF)
        parts.append(dot(mixing, x))
    y_ref[...] = jnp.where(lanes < P_SIZE, parts[0], parts[1])


def inner_backward_kernel(
    x_ref, dy_ref, g_ref, log_ref, log_row_ref, dt_row_ref, sc_ref, sr_ref,
    dx_ref, dg_ref, row_ref, col_ref,
):
    pair = pl.program_id(0)

    @pl.when(pair == 0)
    def _():
        dg_ref[...] = jnp.zeros_like(dg_ref)
        row_ref[...] = jnp.zeros_like(row_ref)

    x = x_ref[...]
    dy = dy_ref[...]
    lanes = lax.broadcasted_iota(jnp.int32, x.shape, 1)
    row_lanes = lax.broadcasted_iota(jnp.int32, row_ref.shape, 1)
    parts = []
    for i in range(2):
        head = 2 * pair + i
        e = decay_between(log_ref, log_row_ref, sc_ref, sr_ref, head)
        dt = dt_row_ref[pl.ds(head, 1), :]
        g = g_ref[...]
        mine = (lanes < P_SIZE) if i == 0 else (lanes >= P_SIZE)
        dm = dot_tb(jnp.where(mine, dy, jnp.zeros_like(dy)), x)
        q = dm * e
        eg = e * g
        parts.append(dot_ta((eg * dt).astype(BF), dy))
        qd = q * dt
        dg_ref[...] += qd
        row_ref[...] += jnp.where(
            row_lanes == head, jnp.sum(qd * g, axis=1, keepdims=True), 0.0
        )
        col_ref[pl.ds(head, 1), :] = jnp.sum(q * g, axis=0, keepdims=True)
    dx_ref[...] = jnp.where(lanes < P_SIZE, parts[0], parts[1])


def whole(shape):
    return pl.BlockSpec(shape, lambda p: (0,) * len(shape))


def pair_block(rows):
    return pl.BlockSpec((rows, 2 * P_SIZE), lambda p: (0, p))


def params():
    return pltpu.CompilerParams(vmem_limit_bytes=VMEM)


def inner_forward(x, g, log_col, log_row, dt_row, seg_col, seg_row):
    t = x.shape[0]
    return pl.pallas_call(
        inner_forward_kernel,
        grid=(H // 2,),
        in_specs=[
            pair_block(t), whole((t, t)), whole((t, H)), whole((H, t)), whole((H, t)),
            whole((t, 1)), whole((1, t)),
        ],
        out_specs=pair_block(t),
        out_shape=jax.ShapeDtypeStruct((t, INNER), F32),
        compiler_params=params(),
        cost_estimate=pl.CostEstimate(
            flops=4 * H * t * t * P_SIZE, bytes_accessed=6 * t * INNER, transcendentals=H * t * t
        ),
    )(x, g, log_col, log_row, dt_row, seg_col, seg_row)


def inner_backward(x, dy, g, log_col, log_row, dt_row, seg_col, seg_row):
    t = x.shape[0]
    return pl.pallas_call(
        inner_backward_kernel,
        grid=(H // 2,),
        in_specs=[
            pair_block(t), pair_block(t), whole((t, t)), whole((t, H)), whole((H, t)),
            whole((H, t)), whole((t, 1)), whole((1, t)),
        ],
        out_specs=[pair_block(t), whole((t, t)), whole((t, H)), whole((H, t))],
        out_shape=[
            jax.ShapeDtypeStruct((t, INNER), F32),
            jax.ShapeDtypeStruct((t, t), F32),
            jax.ShapeDtypeStruct((t, H), F32),
            jax.ShapeDtypeStruct((H, t), F32),
        ],
        compiler_params=params(),
        cost_estimate=pl.CostEstimate(
            flops=8 * H * t * t * P_SIZE, bytes_accessed=8 * t * INNER, transcendentals=H * t * t
        ),
    )(x, dy, g, log_col, log_row, dt_row, seg_col, seg_row)


def head_scores(q, k_ref, allowed, lanes, i):
    mine = (lanes < HD) if i == 0 else (lanes >= HD)
    own = jnp.where(mine, q, jnp.zeros_like(q))
    return mine, own, jnp.where(allowed, dot_tb(own, k_ref[...]) * SCALE, -1e30)


def keys_allowed(first, sc_ref, sr_ref):
    shape = (sc_ref.shape[0], sr_ref.shape[1])
    at_row = lax.broadcasted_iota(jnp.int32, shape, 0) + first
    at_col = lax.broadcasted_iota(jnp.int32, shape, 1)
    return (at_row >= at_col) & (sc_ref[...] == sr_ref[...])


def attend_forward_kernel(q_ref, k_ref, v_ref, sc_ref, sr_ref, out_ref, lse_ref):
    first = lax.axis_index("seq") * q_ref.shape[0]
    allowed = keys_allowed(first, sc_ref, sr_ref)
    q = q_ref[...]
    lanes = lax.broadcasted_iota(jnp.int32, q.shape, 1)
    outs, totals = [], []
    for i in range(2):
        _, _, scores = head_scores(q, k_ref, allowed, lanes, i)
        top = jnp.max(scores, axis=1, keepdims=True)
        probs = jnp.exp(scores - top)
        total = jnp.sum(probs, axis=1, keepdims=True)
        outs.append(dot(probs.astype(BF), v_ref[...]) / total)
        totals.append(top + jnp.log(total))
    out_ref[...] = jnp.where(lanes < HD, outs[0], outs[1]).astype(BF)
    lse_ref[...] = jnp.where(lanes < HD, totals[0], totals[1])


def attend_backward_kernel(
    q_ref, k_ref, v_ref, dm_ref, lse_ref, sc_ref, sr_ref, dq_ref, dk_ref, dv_ref
):
    pair = pl.program_id(0)

    @pl.when(lax.rem(pair, NH // KVH // 2) == 0)
    def _():
        dk_ref[...] = jnp.zeros_like(dk_ref)
        dv_ref[...] = jnp.zeros_like(dv_ref)

    first = lax.axis_index("seq") * q_ref.shape[0]
    allowed = keys_allowed(first, sc_ref, sr_ref)
    q = q_ref[...]
    dmix = dm_ref[...]
    lanes = lax.broadcasted_iota(jnp.int32, q.shape, 1)
    dqs = []
    for i in range(2):
        mine, own, scores = head_scores(q, k_ref, allowed, lanes, i)
        probs = jnp.exp(scores - lse_ref[:, i * HD : i * HD + 1])
        down = jnp.where(mine, dmix, jnp.zeros_like(dmix))
        dp = dot_tb(down, v_ref[...])
        delta = jnp.sum(probs * dp, axis=1, keepdims=True)
        ds = (probs * (dp - delta)).astype(BF)
        dqs.append(dot(ds, k_ref[...]) * SCALE)
        dk_ref[...] += dot_ta(ds, own) * SCALE
        dv_ref[...] += dot_ta(probs.astype(BF), down)
    dq_ref[...] = jnp.where(lanes < HD, dqs[0], dqs[1]).astype(BF)


def kv_block(keys):
    per = NH // KVH // 2
    return pl.BlockSpec((keys, 2 * HD), lambda p: (0, p // per))


def attend_forward(q, k2, v2, seg_col, seg_row):
    t, keys = q.shape[0], k2.shape[0]
    return pl.pallas_call(
        attend_forward_kernel,
        grid=(NH // 2,),
        in_specs=[
            pair_block(t), kv_block(keys), kv_block(keys), whole((t, 1)), whole((1, keys)),
        ],
        out_specs=[pair_block(t), pair_block(t)],
        out_shape=[
            jax.ShapeDtypeStruct((t, NH * HD), BF),
            jax.ShapeDtypeStruct((t, NH * HD), F32),
        ],
        compiler_params=params(),
        cost_estimate=pl.CostEstimate(
            flops=8 * NH * t * keys * HD, bytes_accessed=2 << 20, transcendentals=NH * t * keys
        ),
    )(q, k2, v2, seg_col, seg_row)


def attend_backward(q, k2, v2, dmix, lse, seg_col, seg_row):
    t, keys = q.shape[0], k2.shape[0]
    return pl.pallas_call(
        attend_backward_kernel,
        grid=(NH // 2,),
        in_specs=[
            pair_block(t), kv_block(keys), kv_block(keys), pair_block(t), pair_block(t),
            whole((t, 1)), whole((1, keys)),
        ],
        out_specs=[pair_block(t), kv_block(keys), kv_block(keys)],
        out_shape=[
            jax.ShapeDtypeStruct((t, NH * HD), BF),
            jax.ShapeDtypeStruct((keys, 2 * KVH * HD), F32),
            jax.ShapeDtypeStruct((keys, 2 * KVH * HD), F32),
        ],
        compiler_params=params(),
        cost_estimate=pl.CostEstimate(
            flops=20 * NH * t * keys * HD, bytes_accessed=4 << 20, transcendentals=NH * t * keys
        ),
    )(q, k2, v2, dmix, lse, seg_col, seg_row)


def doubled(pair):
    a, b = pair[:, :HD], pair[:, HD:]
    return jnp.concatenate([a, a, b, b], axis=1)


def folded(wide):
    parts = [wide[:, i * HD : (i + 1) * HD] for i in range(2 * KVH)]
    return jnp.concatenate([parts[0] + parts[1], parts[2] + parts[3]], axis=1)


def carried_states(everything, coefs, size):
    total = 0.0
    for k in range(size):
        part = everything[k].reshape(H, P_SIZE, N).astype(F32)
        total = total + coefs[k][:, None, None] * part
    return total.reshape(INNER, N)


def norm_back(values, scale, gain, grad):
    weighted = gain * grad
    return scale * weighted - values * scale**3 * jnp.mean(
        values * weighted, axis=-1, keepdims=True
    )


def body(
    hidden_in,
    segments,
    cotangent,
    in_proj,
    query_proj,
    key_proj,
    value_proj,
    attn_proj,
    mixer_proj,
    gate_proj,
    up_proj,
    down_proj,
    conv_weight,
    conv_bias,
    norm_one,
    norm_two,
    mixer_norm,
    step_bias,
    decay_log,
    skip_gain,
):
    size, here = lax.axis_size("seq"), lax.axis_index("seq")
    owners = size * lax.axis_size("dp")
    t = hidden_in.shape[1]
    seq_length = segments.shape[1]
    own_conv, own_d, own_in = conv_weight.shape[0], norm_one.shape[0], mixer_norm.shape[0]
    width = own_d * owners

    small = jnp.concatenate(
        [conv_weight.T.reshape(-1), conv_bias, norm_one, norm_two, mixer_norm]
    )
    n_small = small.shape[0]
    extra = -(-n_small // own_d)
    small = jnp.pad(small, (0, extra * own_d - n_small)).reshape(own_d, extra)
    in_pack = gather_all(
        jnp.concatenate(
            [in_proj[:, :Q_AT], query_proj, key_proj, value_proj, in_proj[:, Q_AT:], small], axis=1
        )
    )
    small = in_pack[:, PACK:].reshape(owners, own_d * extra)
    own_rows = [down_proj.shape[0], mixer_proj.shape[0], attn_proj.shape[0]]
    rows_at = [0, own_rows[0], own_rows[0] + own_rows[1], sum(own_rows)]
    tall = gather_all(jnp.concatenate([down_proj, mixer_proj, attn_proj], axis=0))
    tall = tall.reshape(owners, rows_at[3], -1)
    full_down, full_mixer, full_attn = [
        tall[:, rows_at[i] : rows_at[i + 1]].reshape(owners * own_rows[i], -1) for i in range(3)
    ]
    full_gu = gather_all(jnp.concatenate([gate_proj, up_proj], axis=1))

    cut = (CONV + 1) * own_conv
    conv_all = (
        small[:, :cut]
        .reshape(owners, CONV + 1, own_conv)
        .transpose(1, 0, 2)
        .reshape(CONV + 1, CONV_W)
        .astype(F32)
    )
    gains = (
        small[:, cut : cut + 2 * own_d]
        .reshape(owners, 2, own_d)
        .transpose(1, 0, 2)
        .reshape(2, width)
        .astype(F32)
    )
    gain_one, gain_two = gains[0], gains[1]
    mixer_gain = small[:, cut + 2 * own_d : n_small].reshape(INNER).astype(F32)

    segs = segments[0]
    first = here * t
    padded_ids = jnp.concatenate([jnp.full((CONV - 1,), -1, jnp.int32), segs])
    ext_ids = lax.dynamic_slice_in_dim(padded_ids, first, t + CONV - 1, 0)
    ids = ext_ids[CONV - 1 :]
    before = ext_ids[CONV - 2]
    taps = [(ext_ids[j : j + t] == ids).astype(F32)[:, None] for j in range(CONV)]
    seg_col, seg_row, seg_all = ids[:, None], ids[None, :], segs[None, :]
    to_end = (ids == ids[-1]).astype(F32)[:, None]
    from_before = (ids == before).astype(F32)[:, None]
    across = (ids[-1] == before).astype(F32)
    lower = jnp.tril(jnp.ones((t, t), F32))
    spread = jnp.repeat(jnp.eye(H, dtype=F32), P_SIZE, axis=1)

    hidden = hidden_in[0].astype(F32)
    scale_one = lax.rsqrt(jnp.mean(hidden * hidden, axis=-1, keepdims=True) + EPS)
    normed = (hidden * scale_one * gain_one).astype(BF)
    proj = dot(normed, in_pack).astype(BF)
    query = proj[:, Q_AT:K_AT]
    conv_in = proj[:, INNER:Q_AT]
    pairs = [(i, i + 1) for i in range(size - 1)]
    rim = lax.ppermute(conv_in[t - CONV + 1 :], "seq", pairs)
    kv = lax.all_gather(proj[:, K_AT:RAW_AT], "seq", axis=0, tiled=True)
    gate_z = proj[:, :INNER].astype(F32)
    step_in = proj[:, RAW_AT:PACK].astype(F32) + step_bias
    ext = jnp.concatenate([rim, conv_in], axis=0).astype(F32)

    running = conv_all[CONV]
    for j in range(CONV):
        running = running + conv_all[j] * ext[j : j + t] * taps[j]
    conv_sig = jax.nn.sigmoid(running)
    conv_out = running * conv_sig
    x = conv_out[:, :INNER]
    x_low = x.astype(BF)
    write = conv_out[:, INNER : INNER + N].astype(BF)
    read = conv_out[:, INNER + N :].astype(BF)
    dt = jax.nn.softplus(step_in)
    rate = -jnp.exp(decay_log)
    log_decay = exact_dot(lower, dt * rate)
    log_row, dt_row = log_decay.T, dt.T
    end_bare = jnp.exp(log_decay[-1:] - log_decay) * to_end
    end_weight = end_bare * dt
    from_state = jnp.exp(log_decay) * from_before
    wide = exact_dot(jnp.concatenate([end_weight, from_state], axis=0), spread)
    end_wide, from_wide = wide[:t], wide[t:]
    skip_wide = jnp.repeat(skip_gain, P_SIZE)
    xw = (x * end_wide).astype(BF)
    state_local = dot_ta(xw, write)
    block_decay = jnp.exp(log_decay[-1]) * across
    decay_rows = jnp.pad(block_decay[None, :], ((0, 15), (0, N - H)))
    states = lax.all_gather(
        jnp.concatenate([state_local, decay_rows], axis=0).astype(BF), "seq", axis=0
    )
    decays = states[:, INNER, :H].astype(F32)
    ones = jnp.ones((H,), F32)
    fore, back = [None] * size, [None] * size
    run = ones
    for k in range(size - 1, -1, -1):
        inside = k < here
        fore[k] = jnp.where(inside, run, 0.0)
        run = jnp.where(inside, run * decays[k], run)
    run = ones
    for k in range(size):
        inside = k > here
        back[k] = jnp.where(inside, run, 0.0)
        run = jnp.where(inside, run * decays[k], run)
    state_f = carried_states(states[:, :INNER], fore, size)
    state_in = state_f.astype(BF)

    gram = dot_tb(read, write)
    inner = inner_forward(x_low, gram, log_decay, log_row, dt_row, seg_col, seg_row)
    from_read = dot_tb(read, state_in)
    ssm_out = inner + from_wide * from_read + skip_wide * x
    sig_z = jax.nn.sigmoid(gate_z)
    silu_z = gate_z * sig_z
    gated = ssm_out * silu_z
    scale_mix = lax.rsqrt(jnp.mean(gated * gated, axis=-1, keepdims=True) + EPS)
    mixed = (gated * scale_mix * mixer_gain).astype(BF)

    k2, v2 = doubled(kv[:, : KVH * HD]), doubled(kv[:, KVH * HD :])
    attn_mix, lse = attend_forward(query, k2, v2, seg_col, seg_all)
    resid = hidden + dot(mixed, full_mixer) + dot(attn_mix, full_attn)
    scale_two = lax.rsqrt(jnp.mean(resid * resid, axis=-1, keepdims=True) + EPS)
    normed_two = (resid * scale_two * gain_two).astype(BF)
    ff = full_gu.shape[1] // 2
    gate_up = dot(normed_two, full_gu)
    gate_val, up_val = gate_up[:, :ff], gate_up[:, ff:]
    sig_g = jax.nn.sigmoid(gate_val)
    activated = (gate_val * sig_g * up_val).astype(BF)
    layer_out = (resid + dot(activated, full_down)).astype(BF)

    cot = cotangent[0]
    down_w = dot_ta(activated, cot).astype(BF)
    act_grad = dot_tb(cot, full_down)
    gate_grad = act_grad * up_val * sig_g * (1.0 + gate_val * (1.0 - sig_g))
    up_grad = act_grad * gate_val * sig_g
    gu_grad = jnp.concatenate([gate_grad.astype(BF), up_grad.astype(BF)], axis=1)
    gu_w = dot_ta(normed_two, gu_grad).astype(BF)
    normed_two_grad = dot_tb(gu_grad, full_gu)
    two_grad = jnp.sum(resid * scale_two * normed_two_grad, axis=0)
    resid_grad = cot.astype(F32) + norm_back(resid, scale_two, gain_two, normed_two_grad)
    resid_low = resid_grad.astype(BF)
    mixed_grad = dot_tb(resid_low, full_mixer)
    mix_grad = dot_tb(resid_low, full_attn).astype(BF)

    gain_grad = jnp.sum(gated * scale_mix * mixed_grad, axis=0)
    gated_grad = norm_back(gated, scale_mix, mixer_gain, mixed_grad)
    out_grad = gated_grad * silu_z
    gate_z_grad = gated_grad * ssm_out * sig_z * (1.0 + gate_z * (1.0 - sig_z))
    out_low = out_grad.astype(BF)
    out_from = (out_grad * from_wide).astype(BF)
    state_grad = dot_ta(out_from, read).astype(BF)
    state_grads = lax.all_gather(state_grad, "seq", axis=0)

    query_grad, dk2, dv2 = attend_backward(query, k2, v2, mix_grad, lse, seg_col, seg_all)
    kv_grad = lax.psum_scatter(
        jnp.concatenate([folded(dk2), folded(dv2)], axis=1).astype(BF),
        "seq",
        scatter_dimension=0,
        tiled=True,
    )
    mixer_w = dot_ta(mixed, resid_low).astype(BF)
    attn_w = dot_ta(attn_mix, resid_low).astype(BF)
    tall_w = scatter_all(
        jnp.concatenate(
            [w.reshape(owners, -1, w.shape[1]) for w in (down_w, mixer_w, attn_w)], axis=1
        ).reshape(owners * rows_at[3], -1)
    )
    down_w, mixer_w, attn_w = [tall_w[rows_at[i] : rows_at[i + 1]] for i in range(3)]

    inner_x, gram_grad, row_sum, col_sum = inner_backward(
        x_low, out_low, gram, log_decay, log_row, dt_row, seg_col, seg_row
    )
    gram_low = gram_grad.astype(BF)
    skip_grad = jnp.sum(jnp.sum(out_grad * x, axis=0).reshape(H, P_SIZE), axis=1)
    later_f = carried_states(state_grads, back, size)
    later = later_f.astype(BF)
    decay_grad = jnp.sum((later_f * state_f).reshape(H, P_SIZE * N), axis=1)
    from_write = dot_tb(write, later)
    x_grad = inner_x + skip_wide * out_grad + end_wide * from_write
    write_grad = dot_ta(gram_low, read) + dot(xw, later)
    read_grad = dot(gram_low, write) + dot(out_from, state_in)
    sums = exact_dot(
        jnp.concatenate([out_grad * from_read, x * from_write], axis=0), spread.T
    )
    from_grad, end_grad = sums[:t] * from_state, sums[t:]
    end_part = end_weight * end_grad
    dt_part = col_sum.T
    log_grad = row_sum - dt * dt_part + from_grad - end_part
    last = (jnp.arange(t) == t - 1).astype(F32)[:, None]
    log_grad = log_grad + last * (jnp.sum(end_part, axis=0) + block_decay * decay_grad)
    rate_grad = exact_dot(lower.T, log_grad)
    dt_grad = dt_part + end_bare * end_grad + rate_grad * rate
    decay_log_grad = jnp.sum(rate_grad * dt * rate, axis=0)
    raw_grad = dt_grad * jax.nn.sigmoid(step_in)
    step_bias_grad = jnp.sum(raw_grad, axis=0)

    conv_grad = jnp.concatenate([x_grad, write_grad, read_grad], axis=1)
    sum_grad = conv_grad * conv_sig * (1.0 + running * (1.0 - conv_sig))
    conv_b_grad = jnp.sum(sum_grad, axis=0)
    conv_w_grads = []
    ext_grad = 0.0
    for j in range(CONV):
        counted = sum_grad * taps[j]
        conv_w_grads.append(jnp.sum(counted * ext[j : j + t], axis=0))
        ext_grad = ext_grad + jnp.pad(counted * conv_all[j], ((j, CONV - 1 - j), (0, 0)))
    rim_grad = lax.ppermute(ext_grad[: CONV - 1], "seq", [(b, a) for a, b in pairs])
    conv_in_grad = ext_grad[CONV - 1 :] + jnp.pad(rim_grad, ((t - CONV + 1, 0), (0, 0)))
    pack_grad = jnp.concatenate(
        [
            gate_z_grad.astype(BF),
            conv_in_grad.astype(BF),
            query_grad,
            kv_grad,
            raw_grad.astype(BF),
            jnp.zeros((t, extra), BF),
        ],
        axis=1,
    )
    normed_grad = dot_tb(pack_grad, in_pack)
    one_grad = jnp.sum(hidden * scale_one * normed_grad, axis=0)
    input_grad = resid_grad + norm_back(hidden, scale_one, gain_one, normed_grad)

    conv_grads = jnp.stack(conv_w_grads + [conv_b_grad])
    norm_grads = jnp.stack([one_grad, two_grad])
    small_grad = jnp.concatenate(
        [
            conv_grads.reshape(CONV + 1, owners, own_conv).transpose(1, 0, 2).reshape(owners, cut),
            norm_grads.reshape(2, owners, own_d).transpose(1, 0, 2).reshape(owners, 2 * own_d),
            gain_grad.reshape(owners, own_in),
        ],
        axis=1,
    )
    small_grad = jnp.pad(small_grad, ((0, 0), (0, extra * own_d - n_small)))
    pack_w = dot_ta(normed, pack_grad) + jnp.pad(
        small_grad.reshape(width, extra), ((0, 0), (PACK, 0))
    )
    pack_w = pack_w.astype(BF)
    wide_w = scatter_all(jnp.concatenate([gu_w, pack_w], axis=1))
    gu_w, pack_w = wide_w[:, : 2 * ff], wide_w[:, 2 * ff :]
    small_own = pack_w[:, PACK:].reshape(-1)
    head_sums = lax.psum(jnp.stack([step_bias_grad, decay_log_grad, skip_grad]), BOTH)
    taps_cut = CONV * own_conv
    return (
        layer_out[None],
        input_grad[None],
        jnp.concatenate([pack_w[:, :Q_AT], pack_w[:, RAW_AT:PACK]], axis=1),
        pack_w[:, Q_AT:K_AT],
        pack_w[:, K_AT:V_AT],
        pack_w[:, V_AT:RAW_AT],
        attn_w,
        mixer_w,
        gu_w[:, :ff],
        gu_w[:, ff:],
        down_w,
        small_own[:taps_cut].reshape(CONV, own_conv).T,
        small_own[taps_cut:cut],
        small_own[cut : cut + own_d],
        small_own[cut + own_d : cut + 2 * own_d],
        small_own[cut + 2 * own_d : n_small],
        head_sums[0],
        head_sums[1],
        head_sums[2],
    )


def solution(mesh):
    placed = (
        P("dp", "seq", None),
        P("dp", None),
        P("dp", "seq", None),
        P(("dp", "seq"), None),
        P(("dp", "seq"), None),
        P(("dp", "seq"), None),
        P(("dp", "seq"), None),
        P(("dp", "seq"), None),
        P(("dp", "seq"), None),
        P(("dp", "seq"), None),
        P(("dp", "seq"), None),
        P(("dp", "seq"), None),
        P(("dp", "seq"), None),
        P(("dp", "seq")),
        P(("dp", "seq")),
        P(("dp", "seq")),
        P(("dp", "seq")),
        P(),
        P(),
        P(),
    )
    return jax.shard_map(
        body,
        mesh=mesh,
        in_specs=placed,
        out_specs=(
            P("dp", "seq", None),
            P("dp", "seq", None),
            P(("dp", "seq"), None),
            P(("dp", "seq"), None),
            P(("dp", "seq"), None),
            P(("dp", "seq"), None),
            P(("dp", "seq"), None),
            P(("dp", "seq"), None),
            P(("dp", "seq"), None),
            P(("dp", "seq"), None),
            P(("dp", "seq"), None),
            P(("dp", "seq"), None),
            P(("dp", "seq")),
            P(("dp", "seq")),
            P(("dp", "seq")),
            P(("dp", "seq")),
            P(),
            P(),
            P(),
        ),
        check_vma=False,
    )
```
